512 devices in a mesh: section: 64 (over y_hi, z, core), dp: 8 (over y_lo, x).
Axes of the slice: x: 4, y: 8 (y_hi: 4, y_lo: 2; y = y_hi * 2 + y_lo), z: 8, core: 2. Of those that a mesh axis runs over, the one named last changes fastest.
Arguments:
- qkv_weight: bfloat16 [2, 64, 512, 1536], P(None, 'section', 'dp'), may hold values from -0.25 to 0.25
- out_weight: bfloat16 [2, 64, 512, 512], P(None, 'section', 'dp'), may hold values from -0.25 to 0.25
- activations: bfloat16 [2, 64, 8, 128, 512], P(None, 'section', 'dp'), may hold values from -60 to 60
- cotangents: bfloat16 [2, 64, 8, 128, 512], P(None, 'section', 'dp'), may hold values from -6 to 6
- mirrored_stash: bfloat16 [2, 2, 64, 8, 128, 512], P(None, None, 'section', 'dp'), may hold values from -60 to 60
- arrivals: bfloat16 [2, 8, 128, 512], P(None, 'dp'), may hold values from -60 to 60
- head_grads: bfloat16 [2, 8, 128, 512], P(None, 'dp'), may hold values from -6 to 6
Outputs:
- qkv_grad: float32 [2, 64, 512, 1536], P(None, 'section', 'dp')
- out_grad: float32 [2, 64, 512, 512], P(None, 'section', 'dp')
- new_activations: bfloat16 [2, 64, 8, 128, 512], P(None, 'section', 'dp')
- new_cotangents: bfloat16 [2, 64, 8, 128, 512], P(None, 'section', 'dp')
The draws below stay inside these ranges and needn't reach their ends.
Inputs may be any that keep to these rules, and one draw needn't show every extreme that they name: `qkv_weight`: every attention score q k^T / sqrt(64) that the layers form from the given inputs lies within -80 to 80.
All inputs are finite; a program needn't handle non-finite values.
Results may differ from the reference program's by a relative error of at most 0.025.
Values may be sent and summed in bfloat16 or wider, within the bound.
A program may use at most 64 MiB of HBM per device.

```python
import math
import jax
import jax.numpy as jnp
from jax import lax

HEADS = 8
HEAD = 64
D = 512
SEQ = 128
TICKS = 2
SECTIONS = 64
GROUPS = 8


def field_draw(key, shape):
    keys = jax.random.split(key, 5)
    gauss = jnp.clip(jax.random.normal(keys[0], shape, jnp.float32), -4.0, 4.0)
    base = gauss
    row_scale = jnp.exp(jax.random.uniform(keys[3], shape[:-1] + (1,), jnp.float32, minval=math.log(0.3), maxval=math.log(3.0)))
    col_scale = jnp.exp(jax.random.uniform(keys[4], (D,), jnp.float32, minval=math.log(0.3), maxval=math.log(3.0)))
    return (base * row_scale * col_scale).astype(jnp.bfloat16)


def draw_activations(key, part):
    key = jax.random.fold_in(key, 11)
    shape = (2, SECTIONS, GROUPS, SEQ, D)
    return field_draw(key, shape)


def draw_mirrored_stash(key, part):
    key = jax.random.fold_in(key, 23)
    shape = (TICKS, 2, SECTIONS, GROUPS, SEQ, D)
    return field_draw(key, shape)


def draw_arrivals(key, part):
    key = jax.random.fold_in(key, 37)
    shape = (TICKS, GROUPS, SEQ, D)
    return field_draw(key, shape)


def level_of(key, dims, pieces, least, top_value):
    def one(axis_at, shards_of):
        draws = jax.random.uniform(jax.random.fold_in(jax.random.fold_in(key, 6), axis_at), (shards_of,), jnp.float32, least / len(pieces), top_value / len(pieces))
        return jnp.repeat(jnp.exp(draws), dims[axis_at] // shards_of).reshape((-1,) + (1,) * (len(dims) - axis_at - 1))

    gain = one(*pieces[0])
    for cut in pieces[1:]:
        gain = gain * one(*cut)
    return gain


def scatter_about(key, dims, spread, bound, pieces=(), held_as=jnp.bfloat16):
    entries = jax.random.normal(key, dims, jnp.float32) * spread
    if len(pieces) > 0:
        entries = level_of(key, dims, pieces, -0.22, 0.18) * entries
    return jnp.clip(entries, min=-bound, max=bound).astype(held_as)


def setup_inputs(seed: int = 0) -> dict:
    key_list = jax.random.split(jax.random.key(seed), 8)
    qkv_weight = scatter_about(key_list[0], (2, SECTIONS, D, 3 * D), D ** -0.5, 0.25, ((1, 64), (2, 8)))
    out_weight = scatter_about(key_list[1], (2, SECTIONS, D, D), D ** -0.5, 0.25, ((1, 64), (2, 8)))
    activations = draw_activations(jax.random.fold_in(key_list[7], 71), 0)
    cotangents = scatter_about(key_list[3], (2, SECTIONS, GROUPS, SEQ, D), 1.0, 6.0, ((1, 64), (2, 8)))
    mirrored_stash = draw_mirrored_stash(jax.random.fold_in(key_list[7], 71), 0)
    arrivals = draw_arrivals(jax.random.fold_in(key_list[7], 71), 0)
    head_grads = scatter_about(key_list[6], (TICKS, GROUPS, SEQ, D), 1.0, 6.0, ((1, 8),))
    return {"qkv_weight": qkv_weight, "out_weight": out_weight, "activations": activations, "cotangents": cotangents, "mirrored_stash": mirrored_stash, "arrivals": arrivals, "head_grads": head_grads}


def attend(inputs, qkv_part, out_part):
    row_count = inputs.shape[0]
    feat_width = inputs.shape[1]
    floats = inputs.astype(jnp.float32)
    factor = lax.rsqrt(lax.optimization_barrier(jnp.mean(floats * floats, axis=-1, keepdims=True)) + 1e-05)
    normed = (floats * factor).astype(jnp.bfloat16)
    packed = jnp.dot(normed, qkv_part, preferred_element_type=jnp.float32).astype(jnp.bfloat16)
    queries = packed[:, :feat_width].reshape(row_count, HEADS, HEAD).astype(jnp.float32)
    key_rows = packed[:, feat_width:2 * feat_width].reshape(row_count, HEADS, HEAD).astype(jnp.float32)
    values = packed[:, 2 * feat_width:].reshape(row_count, HEADS, HEAD).astype(jnp.float32)
    scores = jnp.einsum('qhd,khd->hqk', queries, key_rows) * HEAD ** (-0.5)
    query_pos = lax.broadcasted_iota(jnp.int32, (row_count, row_count), 0)
    key_pos = lax.broadcasted_iota(jnp.int32, (row_count, row_count), 1)
    causal = (key_pos <= query_pos)[None]
    raised = jnp.where(causal, jnp.exp(scores), jnp.zeros_like(scores))
    soft_weights = (raised / lax.optimization_barrier(jnp.sum(raised, axis=-1, keepdims=True))).astype(jnp.bfloat16)
    context = jnp.einsum('hqk,khd->qhd', soft_weights.astype(jnp.float32), values)
    context = context.astype(jnp.bfloat16).reshape(row_count, feat_width)
    mixed = jnp.dot(context, out_part, preferred_element_type=jnp.float32)
    return (floats + mixed).astype(jnp.bfloat16)

def input_pull(inputs, grads_in, qkv_part, out_part):
    unused, pull = jax.vjp(attend, inputs, qkv_part, out_part)
    return pull(grads_in)[0]

def reference(qkv_weight, out_weight, activations, cotangents, mirrored_stash, arrivals, head_grads):
    layer_count = 2 * SECTIONS
    qkv_all = qkv_weight.reshape(layer_count, D, 3 * D)
    out_all = out_weight.reshape(layer_count, D, D)
    forward_state = activations.reshape(layer_count, GROUPS, SEQ, D)
    back_state = cotangents.reshape(layer_count, GROUPS, SEQ, D)
    stash_all = jnp.roll(mirrored_stash, SECTIONS // 2, axis=2).reshape(TICKS, layer_count, GROUPS, SEQ, D)
    forward_groups = jax.vmap(attend, in_axes=(0, None, None))
    backward_groups = jax.vmap(input_pull, in_axes=(0, 0, None, None))
    for step_index in range(TICKS):
        layer_out = lax.map(lambda items: forward_groups(items[0], items[1], items[2]), (forward_state, qkv_all, out_all))
        forward_state = jnp.concatenate([arrivals[step_index][None], layer_out[:-1]], axis=0)
    history = []
    for step_index in range(TICKS):
        history.append(back_state)
        input_cots = lax.map(lambda items: backward_groups(items[0], items[1], items[2], items[3]), (stash_all[step_index], back_state, qkv_all, out_all))
        back_state = jnp.concatenate([input_cots[1:], head_grads[step_index][None]], axis=0)
    cot_history = jnp.stack(history, axis=1)
    stash_layers = jnp.swapaxes(stash_all, 0, 1)

    def group_total(stash_seq, cot_seq, qkv_part, out_part):
        qkv_sum = jnp.zeros((D, 3 * D), jnp.float32)
        out_sum = jnp.zeros((D, D), jnp.float32)
        for step_index in range(TICKS):
            unused, pull = jax.vjp(attend, stash_seq[step_index], qkv_part, out_part)
            pulled = pull(cot_seq[step_index])
            qkv_sum = qkv_sum + pulled[1].astype(jnp.float32)
            out_sum = out_sum + pulled[2].astype(jnp.float32)
        return (qkv_sum, out_sum)

    def layer_grads(items):
        stash_seq, cot_seq, qkv_part, out_part = items
        qkv_groups, out_groups = jax.vmap(group_total, in_axes=(1, 1, None, None))(stash_seq, cot_seq, qkv_part, out_part)
        qkv_round = lax.optimization_barrier(qkv_groups.astype(jnp.bfloat16))
        out_round = lax.optimization_barrier(out_groups.astype(jnp.bfloat16))
        return (lax.optimization_barrier(jnp.sum(qkv_round.astype(jnp.float32), axis=0)), lax.optimization_barrier(jnp.sum(out_round.astype(jnp.float32), axis=0)))
    qkv_grad, out_grad = lax.map(layer_grads, (stash_layers, cot_history, qkv_all, out_all))
    return (qkv_grad.reshape(2, SECTIONS, D, 3 * D), out_grad.reshape(2, SECTIONS, D, D), forward_state.reshape(2, SECTIONS, GROUPS, SEQ, D), back_state.reshape(2, SECTIONS, GROUPS, SEQ, D))
```

```python
import jax
import jax.numpy as jnp
from jax import lax
from jax.experimental import pallas as pl
from jax.experimental.pallas import tpu as pltpu
from jax.sharding import PartitionSpec as P

MESH = pl.DeviceIdType.MESH
BF = jnp.bfloat16
F32 = jnp.float32
D = 512
SEQ = 128
PAIRS = 4
SHARD = 64
LAYERS = 128


def nn(a, b):
    return lax.dot_general(a, b, (((1,), (0,)), ((), ())), preferred_element_type=F32)


def nt(a, b):
    return lax.dot_general(a, b, (((1,), (1,)), ((), ())), preferred_element_type=F32)


def tn(a, b):
    return lax.dot_general(a, b, (((0,), (0,)), ((), ())), preferred_element_type=F32)


def normalise(x):
    factor = lax.rsqrt(jnp.mean(x * x, axis=-1, keepdims=True) + 1e-05)
    return factor, (x * factor).astype(BF)


def split_heads(low, pair):
    zero = jnp.zeros_like(pair)
    return jnp.concatenate([jnp.where(low, pair, zero), jnp.where(low, zero, pair)], axis=0)


def side_by_side(both):
    return jnp.concatenate([both[:SEQ], both[SEQ:]], axis=1)


def masks():
    low = lax.broadcasted_iota(jnp.int32, (SEQ, SEQ), 1) < 64
    row = lax.broadcasted_iota(jnp.int32, (2 * SEQ, SEQ), 0)
    col = lax.broadcasted_iota(jnp.int32, (2 * SEQ, SEQ), 1)
    return low, col <= lax.rem(row, SEQ)


def attention(low, causal, queries, keys):
    scores = nt(queries, keys) * 0.125
    raised = jnp.where(causal, jnp.exp(scores), 0.0)
    return raised * (1.0 / jnp.sum(raised, axis=-1, keepdims=True))


def lanes(part, pair):
    return pl.ds(pl.multiple_of(part * D + pair * SEQ, SEQ), SEQ)


def forward(x_ref, wq_ref, wo_ref, qkv_ref, ctx_ref, out_ref):
    x = x_ref[...].astype(F32)
    _, normed = normalise(x)
    qkv_ref[...] = nn(normed, wq_ref[...]).astype(BF)
    low, causal = masks()

    def step(pair, carry):
        for g in range(2):
            rows = pl.ds(g * SEQ, SEQ)
            queries = split_heads(low, qkv_ref[rows, lanes(0, pair)])
            soft = attention(low, causal, queries, qkv_ref[rows, lanes(1, pair)]).astype(BF)
            values = split_heads(low, qkv_ref[rows, lanes(2, pair)])
            ctx_ref[rows, lanes(0, pair)] = nn(side_by_side(soft), values).astype(BF)
        return carry

    lax.fori_loop(0, PAIRS, step, 0)
    out_ref[...] = (x + nn(ctx_ref[...], wo_ref[...])).astype(BF)


def backward(
    first, x_ref, cot_ref, wq_ref, wo_ref, qkv_ref, ctx_ref, dctx_ref, dqkv_ref, accq_ref, acco_ref, out_ref
):
    x = x_ref[...].astype(F32)
    factor, normed = normalise(x)
    qkv_ref[...] = nn(normed, wq_ref[...]).astype(BF)
    cot = cot_ref[...]
    dctx_ref[...] = nt(cot, wo_ref[...]).astype(BF)
    low, causal = masks()

    def step(pair, carry):
        for g in range(2):
            rows = pl.ds(g * SEQ, SEQ)
            key_pair = qkv_ref[rows, lanes(1, pair)]
            value_pair = qkv_ref[rows, lanes(2, pair)]
            queries = split_heads(low, qkv_ref[rows, lanes(0, pair)])
            soft = attention(low, causal, queries, key_pair)
            soft_b = soft.astype(BF)
            ctx_ref[rows, lanes(0, pair)] = nn(side_by_side(soft_b), split_heads(low, value_pair)).astype(BF)
            dctx = split_heads(low, dctx_ref[rows, lanes(0, pair)])
            dsoft = nt(dctx, value_pair)
            dqkv_ref[rows, lanes(2, pair)] = tn(soft_b, dctx).astype(BF)
            dscore = soft * (dsoft - jnp.sum(soft * dsoft, axis=-1, keepdims=True))
            dscore = (dscore * 0.125).astype(BF)
            dqkv_ref[rows, lanes(0, pair)] = nn(side_by_side(dscore), split_heads(low, key_pair)).astype(BF)
            dqkv_ref[rows, lanes(1, pair)] = tn(dscore, queries).astype(BF)
        return carry

    lax.fori_loop(0, PAIRS, step, 0)
    dqkv = dqkv_ref[...]
    dnormed = nt(dqkv, wq_ref[...]).astype(BF).astype(F32)
    along = jnp.mean(dnormed * x, axis=-1, keepdims=True)
    dx = factor * dnormed - x * (factor * factor * factor * along)
    out_ref[...] = (cot.astype(F32) + dx).astype(BF)
    dwo = tn(ctx_ref[...], cot)
    dwq = tn(normed, dqkv)
    if first:
        acco_ref[...] = dwo
        accq_ref[...] = dwq
    else:
        acco_ref[...] += dwo
        accq_ref[...] += dwq


def kernel(
    wq_in, wo_in, act_in, cot_in, stash_in, arr_in, head_in,
    qg_out, og_out, na_out, nc_out,
    wq, wo, xs, cs, st, fo, bo, qkv, ctx, dctx, dqkv, accq, acco,
    gsq, gso, grq, gro, g2q, g2o, hgq, hgo, na, nc,
    s_w, r_w, s_f, r_f, s_x, r_x, s_c, r_c, s_st, r_st,
    s_fr, s_br, s_ff, r_ff, s_bf, r_bf, s_g1, r_g1, s_g2, r_g2, s_lo,
):
    s = lax.axis_index("section")
    d = lax.axis_index("dp")
    c = lax.rem(s, 2)
    plane = s // 2
    y = d // 4
    x = lax.rem(d, 4)
    lv = x // 2
    lc = lax.rem(x, 2)
    home = plane * 2 + lc
    layer = lv * 64 + home
    not_first = layer > 0
    not_last = layer < LAYERS - 1

    def worker(number, core, side):
        place = lax.rem(number, 64)
        return (place // 2 * 2 + core, side * 4 + number // 64 * 2 + lax.rem(place, 2))

    def other(device):
        return jnp.logical_or(device[0] != s, device[1] != d)

    sibling = (plane * 2 + 1 - c, d)
    kc = 1 - lax.rem(x, 2)
    up = lax.rem(layer + 1, LAYERS)
    down = lax.rem(layer + LAYERS - 1, LAYERS)
    upper = worker(up, c, y)
    lower = worker(down, c, y)
    group = [y * 4 + 2 * j + 1 - c for j in range(2)]
    shard = [yy * 4 + 2 * i + 1 - c for yy in range(2) for i in range(2)]
    sib_shard = [yy * 4 + 2 * i + c for yy in range(2) for i in range(2)]

    def rows_of(which):
        return pl.ds(pl.multiple_of(which * SHARD, SHARD), SHARD)

    def remote(src, dst, send, recv, device):
        return pltpu.make_async_remote_copy(
            src_ref=src, dst_ref=dst, send_sem=send, recv_sem=recv, device_id=device, device_id_type=MESH
        )

    weight_to = [worker(v * 64 + s, kc, yy) for v in range(2) for yy in range(2)]
    act_to = [worker(v * 64 + s, kc, y) for v in range(2)]
    stash_to = [worker(v * 64 + lax.rem(s + 32, 64), kc, y) for v in range(2)]
    stash_from = [(lax.rem(home + 32, 64), group[j]) for j in range(2)]
    grad_to = [(home, shard[k]) for k in range(4)]
    fwd_to = [(lax.rem(up, 64), group[j]) for j in range(2)]
    bwd_to = [(lax.rem(down, 64), group[j]) for j in range(2)]
    fwd_from = [worker(lax.rem(v * 64 + s + LAYERS - 1, LAYERS), kc, y) for v in range(2)]
    bwd_from = [worker(lax.rem(v * 64 + s + 1, LAYERS), kc, y) for v in range(2)]

    barrier = pltpu.get_barrier_semaphore()

    def greet(device):
        pl.semaphore_signal(barrier, inc=1, device_id=device, device_id_type=MESH)

    greet(sibling)
    for device in grad_to + weight_to + stash_from:
        greet(device)
    greet(lower)
    greet(upper)
    for device in fwd_from + bwd_from:
        pl.when(other(device))(lambda device=device: greet(device))
    greeted = 1 + 8 + 2 + 2
    for device in fwd_to + bwd_to:
        greeted = greeted + other(device).astype(jnp.int32)
    pl.semaphore_wait(barrier, greeted)

    slot = y * 2 + x // 2
    mine = rows_of(d)
    pending = []

    def send(*what):
        copy = remote(*what)
        copy.start()
        pending.append(copy)

    for n in range(4):
        v = n // 2
        send(wq_in.at[v, 0], wq.at[mine], s_w.at[n, 0], r_w.at[slot, 0], weight_to[n])
        send(wo_in.at[v, 0], wo.at[mine], s_w.at[n, 1], r_w.at[slot, 1], weight_to[n])
    j_here = x // 2
    seat = pl.ds(pl.multiple_of(j_here * SEQ, SEQ), SEQ)
    for v in range(2):
        send(act_in.at[v, 0, 0], xs.at[0, seat], s_x.at[v], r_x.at[0, j_here], act_to[v])
    for v in range(2):
        send(cot_in.at[v, 0, 0], cs.at[0, seat], s_c.at[v], r_c.at[0, j_here], act_to[v])

    def early(source, buffers, send_sem, recv_sem, device):
        return remote(source.at[0, 0], buffers.at[1, seat], send_sem, recv_sem.at[1, j_here], device)

    first_head = early(arr_in, xs, s_x.at[2], r_x, act_to[0])
    last_head = early(head_in, cs, s_c.at[2], r_c, act_to[1])
    pl.when(s == 0)(first_head.start)
    pl.when(s == 63)(last_head.start)
    for t in range(2):
        for v in range(2):
            send(
                stash_in.at[t, v, 0, 0], st.at[t, seat], s_st.at[t, v], r_st.at[t, j_here], stash_to[v]
            )

    forwards = []
    for k in range(4):
        rows = rows_of(shard[k])
        for part, ref in ((0, wq), (1, wo)):
            remote(ref.at[rows], ref.at[rows], s_f.at[k, part], r_w.at[k, part], sibling).wait_recv()
            copy = remote(ref.at[rows], ref.at[rows], s_f.at[k, part], r_f.at[k, part], sibling)
            copy.start()
            forwards.append(copy)
    for k in range(4):
        rows = rows_of(sib_shard[k])
        for part, ref in ((0, wq), (1, wo)):
            remote(ref.at[rows], ref.at[rows], s_f.at[k, part], r_f.at[k, part], sibling).wait_recv()

    def half(j):
        return pl.ds(j * SEQ, SEQ)

    def arrive(buffers, recv_sem, t):
        for j in range(2):
            ref = buffers.at[t, half(j)]
            remote(ref, ref, s_lo, recv_sem.at[t, j], sibling).wait_recv()

    def relay(source, buffers, send_sem, recv_sem, device):
        return [
            remote(source.at[0, half(j)], buffers.at[1, half(j)], send_sem.at[j], recv_sem.at[1, j], device)
            for j in range(2)
        ]

    def finish(source, landing, send_sem, recv_sem, devices, number):
        round_ = number // 64
        for j in range(2):
            src = source.at[1, half(j)]
            dst = landing.at[round_]
            copy = remote(src, dst, send_sem.at[j], recv_sem.at[round_], devices[j])
            own = pltpu.make_async_copy(src, dst, recv_sem.at[round_])
            yield copy, own, other(devices[j])

    def start_all(copies, allowed):
        for copy, own, away in copies:
            pl.when(jnp.logical_and(allowed, away))(copy.start)
            pl.when(jnp.logical_and(allowed, jnp.logical_not(away)))(own.start)

    fwd_relay = relay(fo, xs, s_fr, r_x, upper)
    bwd_relay = relay(bo, cs, s_br, r_c, lower)
    fwd_final = list(finish(fo, na, s_ff, r_ff, fwd_to, up))
    bwd_final = list(finish(bo, nc, s_bf, r_bf, bwd_to, down))

    def both(copies, allowed, what):
        def act():
            for copy in copies:
                getattr(copy, what)()

        pl.when(allowed)(act)

    arrive(xs, r_x, 0)
    forward(xs.at[0], wq, wo, qkv, ctx, fo.at[0])
    both(fwd_relay, not_last, "start")
    arrive(xs, r_x, 1)
    forward(xs.at[1], wq, wo, qkv, ctx, fo.at[1])
    start_all(fwd_final, not_last)

    arrive(cs, r_c, 0)
    arrive(st, r_st, 0)
    backward(True, st.at[0], cs.at[0], wq, wo, qkv, ctx, dctx, dqkv, accq, acco, bo.at[0])
    both(bwd_relay, not_first, "start")
    arrive(cs, r_c, 1)
    arrive(st, r_st, 1)
    backward(False, st.at[1], cs.at[1], wq, wo, qkv, ctx, dctx, dqkv, accq, acco, bo.at[1])
    start_all(bwd_final, not_first)

    for k in range(4):
        rows = rows_of(sib_shard[k])
        gsq[k] = accq[rows, :].astype(BF)
        gso[k] = acco[rows, :].astype(BF)
        send(gsq.at[k], grq.at[k], s_g1.at[k, 0], r_g1.at[k, 0], sibling)
        send(gso.at[k], gro.at[k], s_g1.at[k, 1], r_g1.at[k, 1], sibling)
    for k in range(4):
        rows = rows_of(shard[k])
        remote(gsq.at[k], grq.at[k], s_g1.at[k, 0], r_g1.at[k, 0], sibling).wait_recv()
        remote(gso.at[k], gro.at[k], s_g1.at[k, 1], r_g1.at[k, 1], sibling).wait_recv()
        g2q[k] = (accq[rows, :] + grq[k].astype(F32)).astype(BF)
        g2o[k] = (acco[rows, :] + gro[k].astype(F32)).astype(BF)
        send(g2q.at[k], hgq.at[lv, y], s_g2.at[k, 0], r_g2.at[lv, y, 0], grad_to[k])
        send(g2o.at[k], hgo.at[lv, y], s_g2.at[k, 1], r_g2.at[lv, y, 1], grad_to[k])

    own_arrival = pltpu.make_async_copy(arr_in.at[1, 0], na.at[0], r_ff.at[0])
    own_head = pltpu.make_async_copy(head_in.at[1, 0], nc.at[1], r_bf.at[1])
    pl.when(s == 0)(own_arrival.start)
    pl.when(s == 63)(own_head.start)
    for v in range(2):
        pltpu.make_async_copy(arr_in.at[1, 0], na.at[v], r_ff.at[v]).wait()
        na_out[v, 0, 0] = na[v]
        pltpu.make_async_copy(head_in.at[1, 0], nc.at[v], r_bf.at[v]).wait()
        nc_out[v, 0, 0] = nc[v]
    for v in range(2):
        for yy in range(2):
            remote(g2q.at[0], hgq.at[v, yy], s_g2.at[0, 0], r_g2.at[v, yy, 0], sibling).wait_recv()
            remote(g2o.at[0], hgo.at[v, yy], s_g2.at[0, 1], r_g2.at[v, yy, 1], sibling).wait_recv()
        qg_out[v, 0] = hgq[v, 0].astype(F32) + hgq[v, 1].astype(F32)
        og_out[v, 0] = hgo[v, 0].astype(F32) + hgo[v, 1].astype(F32)

    for copy in pending + forwards:
        copy.wait_send()
    pl.when(s == 0)(first_head.wait_send)
    pl.when(s == 63)(last_head.wait_send)
    both(fwd_relay, not_last, "wait_send")
    both(bwd_relay, not_first, "wait_send")
    for copies, allowed in ((fwd_final, not_last), (bwd_final, not_first)):
        for copy, own, away in copies:
            pl.when(jnp.logical_and(allowed, away))(copy.wait_send)


def shards(qkv_weight, out_weight, activations, cotangents, mirrored_stash, arrivals, head_grads):
    dma = pltpu.SemaphoreType.DMA
    hbm = pl.BlockSpec(memory_space=pl.ANY)
    vmem = pl.BlockSpec(memory_space=pltpu.VMEM)
    return pl.pallas_call(
        kernel,
        out_shape=(
            jax.ShapeDtypeStruct((2, 1, SHARD, 3 * D), F32),
            jax.ShapeDtypeStruct((2, 1, SHARD, D), F32),
            jax.ShapeDtypeStruct((2, 1, 1, SEQ, D), BF),
            jax.ShapeDtypeStruct((2, 1, 1, SEQ, D), BF),
        ),
        in_specs=[hbm] * 7,
        out_specs=[vmem] * 4,
        scratch_shapes=[
            pltpu.VMEM((D, 3 * D), BF),
            pltpu.VMEM((D, D), BF),
            pltpu.VMEM((2, 2 * SEQ, D), BF),
            pltpu.VMEM((2, 2 * SEQ, D), BF),
            pltpu.VMEM((2, 2 * SEQ, D), BF),
            pltpu.VMEM((2, 2 * SEQ, D), BF),
            pltpu.VMEM((2, 2 * SEQ, D), BF),
            pltpu.VMEM((2 * SEQ, 3 * D), BF),
            pltpu.VMEM((2 * SEQ, D), BF),
            pltpu.VMEM((2 * SEQ, D), BF),
            pltpu.VMEM((2 * SEQ, 3 * D), BF),
            pltpu.VMEM((D, 3 * D), F32),
            pltpu.VMEM((D, D), F32),
            pltpu.VMEM((4, SHARD, 3 * D), BF),
            pltpu.VMEM((4, SHARD, D), BF),
            pltpu.VMEM((4, SHARD, 3 * D), BF),
            pltpu.VMEM((4, SHARD, D), BF),
            pltpu.VMEM((4, SHARD, 3 * D), BF),
            pltpu.VMEM((4, SHARD, D), BF),
            pltpu.VMEM((2, 2, SHARD, 3 * D), BF),
            pltpu.VMEM((2, 2, SHARD, D), BF),
            pltpu.VMEM((2, SEQ, D), BF),
            pltpu.VMEM((2, SEQ, D), BF),
            dma((4, 2)), dma((4, 2)),
            dma((4, 2)), dma((4, 2)),
            dma((3,)), dma((2, 2)),
            dma((3,)), dma((2, 2)),
            dma((2, 2)), dma((2, 2)),
            dma((2,)), dma((2,)),
            dma((2,)), dma((2,)),
            dma((2,)), dma((2,)),
            dma((4, 2)), dma((4, 2)),
            dma((4, 2)), dma((2, 2, 2)),
            dma,
        ],
        compiler_params=pltpu.CompilerParams(
            collective_id=0, has_side_effects=True, vmem_limit_bytes=48 * 1024 * 1024
        ),
        cost_estimate=pl.CostEstimate(flops=5_000_000_000, bytes_accessed=8_000_000, transcendentals=2_000_000),
        name="window",
    )(qkv_weight, out_weight, activations, cotangents, mirrored_stash, arrivals, head_grads)


def solution(mesh):
    return jax.shard_map(
        shards,
        mesh=mesh,
        in_specs=(
            P(None, "section", "dp", None),
            P(None, "section", "dp", None),
            P(None, "section", "dp", None, None),
            P(None, "section", "dp", None, None),
            P(None, None, "section", "dp", None, None),
            P(None, "dp", None, None),
            P(None, "dp", None, None),
        ),
        out_specs=(
            P(None, "section", "dp", None),
            P(None, "section", "dp", None),
            P(None, "section", "dp", None, None),
            P(None, "section", "dp", None, None),
        ),
        check_vma=False,
    )
```

```python
import jax
import jax.numpy as jnp
from jax import lax
from jax.experimental import pallas as pl
from jax.experimental.pallas import tpu as pltpu
from jax.sharding import PartitionSpec as P

MESH = pl.DeviceIdType.MESH
BF = jnp.bfloat16
F32 = jnp.float32
D = 512
SEQ = 128
PAIRS = 4
SHARD = 64
LAYERS = 128


def nn(a, b):
    return lax.dot_general(a, b, (((1,), (0,)), ((), ())), preferred_element_type=F32)


def nt(a, b):
    return lax.dot_general(a, b, (((1,), (1,)), ((), ())), preferred_element_type=F32)


def tn(a, b):
    return lax.dot_general(a, b, (((0,), (0,)), ((), ())), preferred_element_type=F32)


def normalise(x):
    factor = lax.rsqrt(jnp.mean(x * x, axis=-1, keepdims=True) + 1e-05)
    return factor, (x * factor).astype(BF)


def split_heads(low, pair):
    zero = jnp.zeros_like(pair)
    return jnp.concatenate([jnp.where(low, pair, zero), jnp.where(low, zero, pair)], axis=0)


def side_by_side(both):
    return jnp.concatenate([both[:SEQ], both[SEQ:]], axis=1)


def masks():
    low = lax.broadcasted_iota(jnp.int32, (SEQ, SEQ), 1) < 64
    row = lax.broadcasted_iota(jnp.int32, (2 * SEQ, SEQ), 0)
    col = lax.broadcasted_iota(jnp.int32, (2 * SEQ, SEQ), 1)
    return low, col <= lax.rem(row, SEQ)


def attention(low, causal, queries, keys):
    scores = nt(queries, keys) * 0.125
    raised = jnp.where(causal, jnp.exp(scores), 0.0)
    return raised * (1.0 / jnp.sum(raised, axis=-1, keepdims=True))


def lanes(part, pair):
    return pl.ds(pl.multiple_of(part * D + pair * SEQ, SEQ), SEQ)


def forward(x_ref, wq_ref, wo_ref, qkv_ref, ctx_ref, out_ref):
    x = x_ref[...].astype(F32)
    _, normed = normalise(x)
    qkv_ref[...] = nn(normed, wq_ref[...]).astype(BF)
    low, causal = masks()

    def step(pair, carry):
        for g in range(2):
            rows = pl.ds(g * SEQ, SEQ)
            queries = split_heads(low, qkv_ref[rows, lanes(0, pair)])
            soft = attention(low, causal, queries, qkv_ref[rows, lanes(1, pair)]).astype(BF)
            values = split_heads(low, qkv_ref[rows, lanes(2, pair)])
            ctx_ref[rows, lanes(0, pair)] = nn(side_by_side(soft), values).astype(BF)
        return carry

    lax.fori_loop(0, PAIRS, step, 0)
    out_ref[...] = (x + nn(ctx_ref[...], wo_ref[...])).astype(BF)


def backward(x_ref, cot_ref, wait_cot, wq_ref, wo_ref, qkv_ref, ctx_ref, dctx_ref, dqkv_ref, nrm_ref):
    _, normed = normalise(x_ref[...].astype(F32))
    nrm_ref[...] = normed
    qkv_ref[...] = nn(normed, wq_ref[...]).astype(BF)
    wait_cot()
    dctx_ref[...] = nt(cot_ref[...], wo_ref[...]).astype(BF)
    low, causal = masks()

    def step(pair, carry):
        for g in range(2):
            rows = pl.ds(g * SEQ, SEQ)
            key_pair = qkv_ref[rows, lanes(1, pair)]
            value_pair = qkv_ref[rows, lanes(2, pair)]
            queries = split_heads(low, qkv_ref[rows, lanes(0, pair)])
            soft = attention(low, causal, queries, key_pair)
            soft_b = soft.astype(BF)
            ctx_ref[rows, lanes(0, pair)] = nn(side_by_side(soft_b), split_heads(low, value_pair)).astype(BF)
            dctx = split_heads(low, dctx_ref[rows, lanes(0, pair)])
            dsoft = nt(dctx, value_pair)
            dqkv_ref[rows, lanes(2, pair)] = tn(soft_b, dctx).astype(BF)
            dscore = soft * (dsoft - jnp.sum(soft * dsoft, axis=-1, keepdims=True))
            dscore = (dscore * 0.125).astype(BF)
            dqkv_ref[rows, lanes(0, pair)] = nn(side_by_side(dscore), split_heads(low, key_pair)).astype(BF)
            dqkv_ref[rows, lanes(1, pair)] = tn(dscore, queries).astype(BF)
        return carry

    lax.fori_loop(0, PAIRS, step, 0)


def input_cotangent(x_ref, cot_ref, wq_ref, dqkv_ref, out_ref):
    x = x_ref[...].astype(F32)
    factor, _ = normalise(x)
    dnormed = nt(dqkv_ref[...], wq_ref[...]).astype(BF).astype(F32)
    along = jnp.mean(dnormed * x, axis=-1, keepdims=True)
    dx = factor * dnormed - x * (factor * factor * factor * along)
    out_ref[...] = (cot_ref[...].astype(F32) + dx).astype(BF)


def kernel(
    wq_in, wo_in, act_in, cot_in, stash_in, arr_in, head_in,
    hgq, hgo, na, nc,
    wq, wo, xs, cs, st, fo, bo, qkv, ctx, dctx, dqkv, nrm, accq, acco,
    gsq, gso, grq, gro, g2q, g2o,
    s_w, r_w, s_f, r_f, s_x, r_x, s_c, r_c, s_st, r_st,
    s_fr, s_br, s_ff, r_ff, s_bf, r_bf, s_g1, r_g1, s_g2, r_g2, s_lo, ans_relay, ans_final,
):
    s = lax.axis_index("section")
    d = lax.axis_index("dp")
    c = lax.rem(s, 2)
    plane = s // 2
    y = d // 4
    x = lax.rem(d, 4)
    lv = x // 2
    lc = lax.rem(x + y, 2)
    home = plane * 2 + lc
    layer = lv * 64 + home
    not_first = layer > 0
    not_last = layer < LAYERS - 1

    def worker(number, core, side):
        place = lax.rem(number, 64)
        return (place // 2 * 2 + core, side * 4 + number // 64 * 2 + lax.rem(place + side, 2))

    def other(device):
        return jnp.logical_or(device[0] != s, device[1] != d)

    sibling = (plane * 2 + 1 - c, d)
    kc = 1 - lax.rem(x + y, 2)
    up = lax.rem(layer + 1, LAYERS)
    down = lax.rem(layer + LAYERS - 1, LAYERS)
    upper = worker(up, c, y)
    lower = worker(down, c, y)
    group = [y * 4 + 2 * j + lax.rem(1 - c + y, 2) for j in range(2)]
    shard = [yy * 4 + 2 * i + lax.rem(1 - c + yy, 2) for yy in range(2) for i in range(2)]
    sib_shard = [yy * 4 + 2 * i + lax.rem(c + yy, 2) for yy in range(2) for i in range(2)]

    def rows_of(which):
        return pl.ds(pl.multiple_of(which * SHARD, SHARD), SHARD)

    def remote(src, dst, send, recv, device):
        return pltpu.make_async_remote_copy(
            src_ref=src, dst_ref=dst, send_sem=send, recv_sem=recv, device_id=device, device_id_type=MESH
        )

    weight_to = [worker(v * 64 + s, kc, yy) for v in range(2) for yy in range(2)]
    act_to = [worker(v * 64 + s, kc, y) for v in range(2)]
    stash_to = [worker(v * 64 + lax.rem(s + 32, 64), kc, y) for v in range(2)]
    stash_from = [(lax.rem(home + 32, 64), group[j]) for j in range(2)]
    grad_to = [(home, shard[k]) for k in range(4)]
    fwd_to = [(lax.rem(up, 64), group[j]) for j in range(2)]
    bwd_to = [(lax.rem(down, 64), group[j]) for j in range(2)]
    fwd_from = [worker(lax.rem(v * 64 + s + LAYERS - 1, LAYERS), kc, y) for v in range(2)]
    bwd_from = [worker(lax.rem(v * 64 + s + 1, LAYERS), kc, y) for v in range(2)]

    barrier = pltpu.get_barrier_semaphore()

    def greet(device):
        pl.semaphore_signal(barrier, inc=1, device_id=device, device_id_type=MESH)

    greet(sibling)
    for device in grad_to + weight_to + stash_from:
        greet(device)
    greet(lower)
    greeted = 1 + 8 + 2 + 1
    for ours, theirs in zip(fwd_from + bwd_to, fwd_to + bwd_from):
        pl.when(other(ours))(lambda device=ours: greet(device))
        greeted = greeted + other(theirs).astype(jnp.int32)
    pl.semaphore_wait(barrier, greeted)

    def answer(sem, device):
        pl.semaphore_signal(sem, inc=1, device_id=device, device_id_type=MESH)

    answer(ans_relay, upper)
    for device in bwd_from:
        pl.when(other(device))(lambda device=device: answer(ans_final, device))

    slot = y * 2 + x // 2
    mine = rows_of(d)
    pending = []

    def send(*what):
        copy = remote(*what)
        copy.start()
        pending.append(copy)

    for n in range(4):
        v = n // 2
        send(wq_in.at[v, 0], wq.at[mine], s_w.at[n, 0], r_w.at[slot, 0], weight_to[n])
        send(wo_in.at[v, 0], wo.at[mine], s_w.at[n, 1], r_w.at[slot, 1], weight_to[n])
    j_here = x // 2
    seat = pl.ds(pl.multiple_of(j_here * SEQ, SEQ), SEQ)
    for v in range(2):
        send(act_in.at[v, 0, 0], xs.at[0, seat], s_x.at[v], r_x.at[0, j_here], act_to[v])
    for v in range(2):
        send(cot_in.at[v, 0, 0], cs.at[0, seat], s_c.at[v], r_c.at[0, j_here], act_to[v])

    def early(source, buffers, send_sem, recv_sem, device):
        return remote(source.at[0, 0], buffers.at[1, seat], send_sem, recv_sem.at[1, j_here], device)

    first_head = early(arr_in, xs, s_x.at[2], r_x, act_to[0])
    last_head = early(head_in, cs, s_c.at[2], r_c, act_to[1])
    pl.when(s == 0)(first_head.start)
    pl.when(s == 63)(last_head.start)
    for t in range(2):
        for v in range(2):
            send(
                stash_in.at[t, v, 0, 0], st.at[t, seat], s_st.at[t, v], r_st.at[t, j_here], stash_to[v]
            )

    forwards = []
    for k in range(4):
        rows = rows_of(shard[k])
        for part, ref in ((0, wq), (1, wo)):
            remote(ref.at[rows], ref.at[rows], s_f.at[k, part], r_w.at[k, part], sibling).wait_recv()
            copy = remote(ref.at[rows], ref.at[rows], s_f.at[k, part], r_f.at[k, part], sibling)
            copy.start()
            forwards.append(copy)
    for k in range(4):
        rows = rows_of(sib_shard[k])
        for part, ref in ((0, wq), (1, wo)):
            remote(ref.at[rows], ref.at[rows], s_f.at[k, part], r_f.at[k, part], sibling).wait_recv()

    def half(j):
        return pl.ds(j * SEQ, SEQ)

    def arrive(buffers, recv_sem, t):
        for j in range(2):
            ref = buffers.at[t, half(j)]
            remote(ref, ref, s_lo, recv_sem.at[t, j], sibling).wait_recv()

    def relay(source, buffers, send_sem, recv_sem, device):
        return [
            remote(source.at[0, half(j)], buffers.at[1, half(j)], send_sem.at[j], recv_sem.at[1, j], device)
            for j in range(2)
        ]

    def finish(source, landing, send_sem, recv_sem, devices, number):
        round_ = number // 64
        for j in range(2):
            src = source.at[1, half(j)]
            dst = landing.at[round_]
            copy = remote(src, dst, send_sem.at[j], recv_sem.at[round_], devices[j])
            own = pltpu.make_async_copy(src, dst, recv_sem.at[round_])
            yield copy, own, other(devices[j])

    def start_all(copies, allowed):
        for copy, own, away in copies:
            pl.when(jnp.logical_and(allowed, away))(copy.start)
            pl.when(jnp.logical_and(allowed, jnp.logical_not(away)))(own.start)

    fwd_relay = relay(fo, xs, s_fr, r_x, upper)
    bwd_relay = relay(bo, cs, s_br, r_c, lower)
    fwd_final = list(finish(fo, na, s_ff, r_ff, fwd_to, up))
    bwd_final = list(finish(bo, nc, s_bf, r_bf, bwd_to, down))

    def both(copies, allowed, what):
        def act():
            for copy in copies:
                getattr(copy, what)()

        pl.when(allowed)(act)

    def arrive_cot(t):
        return lambda: arrive(cs, r_c, t)

    work = (wq, wo, qkv, ctx, dctx, dqkv, nrm)

    arrive(xs, r_x, 0)
    forward(xs.at[0], wq, wo, qkv, ctx, fo.at[0])
    both(fwd_relay, not_last, "start")
    arrive(st, r_st, 0)
    backward(st.at[0], cs.at[0], arrive_cot(0), *work)
    input_cotangent(st.at[0], cs.at[0], wq, dqkv, bo.at[0])
    pl.semaphore_wait(ans_relay, 1)
    both(bwd_relay, not_first, "start")
    acco[...] = tn(ctx[...], cs[0])
    accq[...] = tn(nrm[...], dqkv[...])

    arrive(xs, r_x, 1)
    forward(xs.at[1], wq, wo, qkv, ctx, fo.at[1])
    start_all(fwd_final, not_last)
    arrive(st, r_st, 1)
    backward(st.at[1], cs.at[1], arrive_cot(1), *work)
    acco[...] += tn(ctx[...], cs[1])
    accq[...] += tn(nrm[...], dqkv[...])

    for k in range(4):
        rows = rows_of(sib_shard[k])
        gsq[k] = accq[rows, :].astype(BF)
        gso[k] = acco[rows, :].astype(BF)
        send(gsq.at[k], grq.at[k], s_g1.at[k, 0], r_g1.at[k, 0], sibling)
        send(gso.at[k], gro.at[k], s_g1.at[k, 1], r_g1.at[k, 1], sibling)
    for k in range(4):
        rows = rows_of(shard[k])
        remote(gsq.at[k], grq.at[k], s_g1.at[k, 0], r_g1.at[k, 0], sibling).wait_recv()
        remote(gso.at[k], gro.at[k], s_g1.at[k, 1], r_g1.at[k, 1], sibling).wait_recv()
        g2q[k] = (accq[rows, :] + grq[k].astype(F32)).astype(BF)
        g2o[k] = (acco[rows, :] + gro[k].astype(F32)).astype(BF)
        send(g2q.at[k], hgq.at[lv, y], s_g2.at[k, 0], r_g2.at[lv, y, 0], grad_to[k])
        send(g2o.at[k], hgo.at[lv, y], s_g2.at[k, 1], r_g2.at[lv, y, 1], grad_to[k])

    input_cotangent(st.at[1], cs.at[1], wq, dqkv, bo.at[1])
    pl.semaphore_wait(ans_final, sum(other(device).astype(jnp.int32) for device in bwd_to))
    start_all(bwd_final, not_first)

    own_arrival = pltpu.make_async_copy(arr_in.at[1, 0], na.at[0], r_ff.at[0])
    own_head = pltpu.make_async_copy(head_in.at[1, 0], nc.at[1], r_bf.at[1])
    pl.when(s == 0)(own_arrival.start)
    pl.when(s == 63)(own_head.start)
    for v in range(2):
        pltpu.make_async_copy(arr_in.at[1, 0], na.at[v], r_ff.at[v]).wait()
        pltpu.make_async_copy(head_in.at[1, 0], nc.at[v], r_bf.at[v]).wait()
    for v in range(2):
        for yy in range(2):
            remote(g2q.at[0], hgq.at[v, yy], s_g2.at[0, 0], r_g2.at[v, yy, 0], sibling).wait_recv()
            remote(g2o.at[0], hgo.at[v, yy], s_g2.at[0, 1], r_g2.at[v, yy, 1], sibling).wait_recv()

    for copy in pending + forwards:
        copy.wait_send()
    pl.when(s == 0)(first_head.wait_send)
    pl.when(s == 63)(last_head.wait_send)
    both(fwd_relay, not_last, "wait_send")
    both(bwd_relay, not_first, "wait_send")
    for copies, allowed in ((fwd_final, not_last), (bwd_final, not_first)):
        for copy, own, away in copies:
            pl.when(jnp.logical_and(allowed, away))(copy.wait_send)


def hand_over(hgq, hgo, na, nc, qkv_grad, out_grad, new_act, new_cot):
    for v in range(2):
        qkv_grad[v, 0] = hgq[v, 0].astype(F32) + hgq[v, 1].astype(F32)
        out_grad[v, 0] = hgo[v, 0].astype(F32) + hgo[v, 1].astype(F32)
        new_act[v, 0, 0] = na[v]
        new_cot[v, 0, 0] = nc[v]


def shards(qkv_weight, out_weight, activations, cotangents, mirrored_stash, arrivals, head_grads):
    dma = pltpu.SemaphoreType.DMA
    hbm = pl.BlockSpec(memory_space=pl.ANY)
    vmem = pl.BlockSpec(memory_space=pltpu.VMEM)
    results = pl.pallas_call(
        kernel,
        out_shape=(
            jax.ShapeDtypeStruct((2, 2, SHARD, 3 * D), BF),
            jax.ShapeDtypeStruct((2, 2, SHARD, D), BF),
            jax.ShapeDtypeStruct((2, SEQ, D), BF),
            jax.ShapeDtypeStruct((2, SEQ, D), BF),
        ),
        in_specs=[hbm] * 7,
        out_specs=[hbm] * 4,
        scratch_shapes=[
            pltpu.VMEM((D, 3 * D), BF),
            pltpu.VMEM((D, D), BF),
            pltpu.VMEM((2, 2 * SEQ, D), BF),
            pltpu.VMEM((2, 2 * SEQ, D), BF),
            pltpu.VMEM((2, 2 * SEQ, D), BF),
            pltpu.VMEM((2, 2 * SEQ, D), BF),
            pltpu.VMEM((2, 2 * SEQ, D), BF),
            pltpu.VMEM((2 * SEQ, 3 * D), BF),
            pltpu.VMEM((2 * SEQ, D), BF),
            pltpu.VMEM((2 * SEQ, D), BF),
            pltpu.VMEM((2 * SEQ, 3 * D), BF),
            pltpu.VMEM((2 * SEQ, D), BF),
            pltpu.VMEM((D, 3 * D), F32),
            pltpu.VMEM((D, D), F32),
            pltpu.VMEM((4, SHARD, 3 * D), BF),
            pltpu.VMEM((4, SHARD, D), BF),
            pltpu.VMEM((4, SHARD, 3 * D), BF),
            pltpu.VMEM((4, SHARD, D), BF),
            pltpu.VMEM((4, SHARD, 3 * D), BF),
            pltpu.VMEM((4, SHARD, D), BF),
            dma((4, 2)), dma((4, 2)),
            dma((4, 2)), dma((4, 2)),
            dma((3,)), dma((2, 2)),
            dma((3,)), dma((2, 2)),
            dma((2, 2)), dma((2, 2)),
            dma((2,)), dma((2,)),
            dma((2,)), dma((2,)),
            dma((2,)), dma((2,)),
            dma((4, 2)), dma((4, 2)),
            dma((4, 2)), dma((2, 2, 2)),
            dma,
            pltpu.SemaphoreType.REGULAR,
            pltpu.SemaphoreType.REGULAR,
        ],
        compiler_params=pltpu.CompilerParams(
            collective_id=0, has_side_effects=True, vmem_limit_bytes=62 * 1024 * 1024
        ),
        cost_estimate=pl.CostEstimate(flops=5_000_000_000, bytes_accessed=8_000_000, transcendentals=2_000_000),
        name="window",
    )(qkv_weight, out_weight, activations, cotangents, mirrored_stash, arrivals, head_grads)
    return pl.pallas_call(
        hand_over,
        out_shape=(
            jax.ShapeDtypeStruct((2, 1, SHARD, 3 * D), F32),
            jax.ShapeDtypeStruct((2, 1, SHARD, D), F32),
            jax.ShapeDtypeStruct((2, 1, 1, SEQ, D), BF),
            jax.ShapeDtypeStruct((2, 1, 1, SEQ, D), BF),
        ),
        in_specs=[vmem] * 4,
        out_specs=[vmem] * 4,
        name="hand_over",
    )(*results)


def solution(mesh):
    return jax.shard_map(
        shards,
        mesh=mesh,
        in_specs=(
            P(None, "section", "dp", None),
            P(None, "section", "dp", None),
            P(None, "section", "dp", None, None),
            P(None, "section", "dp", None, None),
            P(None, None, "section", "dp", None, None),
            P(None, "dp", None, None),
            P(None, "dp", None, None),
        ),
        out_specs=(
            P(None, "section", "dp", None),
            P(None, "section", "dp", None),
            P(None, "section", "dp", None, None),
            P(None, "section", "dp", None, None),
        ),
        check_vma=False,
    )
```

```python
import jax
import jax.numpy as jnp
from jax import lax
from jax.experimental import pallas as pl
from jax.experimental.pallas import tpu as pltpu
from jax.sharding import PartitionSpec as P

MESH = pl.DeviceIdType.MESH
BF = jnp.bfloat16
F32 = jnp.float32
D = 512
SEQ = 128
PAIRS = 4
SHARD = 64
LAYERS = 128


def nn(a, b):
    return lax.dot_general(a, b, (((1,), (0,)), ((), ())), preferred_element_type=F32)


def nt(a, b):
    return lax.dot_general(a, b, (((1,), (1,)), ((), ())), preferred_element_type=F32)


def tn(a, b):
    return lax.dot_general(a, b, (((0,), (0,)), ((), ())), preferred_element_type=F32)


def normalise(x):
    factor = lax.rsqrt(jnp.mean(x * x, axis=-1, keepdims=True) + 1e-05)
    return factor, (x * factor).astype(BF)


def split_heads(low, pair):
    zero = jnp.zeros_like(pair)
    return jnp.concatenate([jnp.where(low, pair, zero), jnp.where(low, zero, pair)], axis=0)


def side_by_side(both):
    return jnp.concatenate([both[:SEQ], both[SEQ:]], axis=1)


def masks():
    low = lax.broadcasted_iota(jnp.int32, (SEQ, SEQ), 1) < 64
    row = lax.broadcasted_iota(jnp.int32, (2 * SEQ, SEQ), 0)
    col = lax.broadcasted_iota(jnp.int32, (2 * SEQ, SEQ), 1)
    return low, col <= lax.rem(row, SEQ)


def attention(low, causal, queries, keys):
    scores = nt(queries, keys) * 0.125
    raised = jnp.where(causal, jnp.exp(scores), 0.0)
    return raised * (1.0 / jnp.sum(raised, axis=-1, keepdims=True))


def lanes(part, pair):
    return pl.ds(pl.multiple_of(part * D + pair * SEQ, SEQ), SEQ)


def forward(x_ref, wq_ref, wo_ref, qkv_ref, ctx_ref, out_ref):
    x = x_ref[...].astype(F32)
    _, normed = normalise(x)
    qkv_ref[...] = nn(normed, wq_ref[...]).astype(BF)
    low, causal = masks()

    def step(pair, carry):
        for g in range(2):
            rows = pl.ds(g * SEQ, SEQ)
            queries = split_heads(low, qkv_ref[rows, lanes(0, pair)])
            soft = attention(low, causal, queries, qkv_ref[rows, lanes(1, pair)]).astype(BF)
            values = split_heads(low, qkv_ref[rows, lanes(2, pair)])
            ctx_ref[rows, lanes(0, pair)] = nn(side_by_side(soft), values).astype(BF)
        return carry

    lax.fori_loop(0, PAIRS, step, 0)
    out_ref[...] = (x + nn(ctx_ref[...], wo_ref[...])).astype(BF)


def backward(x_ref, cot_ref, wait_cot, wq_ref, wo_ref, qkv_ref, ctx_ref, dctx_ref, dqkv_ref, nrm_ref):
    _, normed = normalise(x_ref[...].astype(F32))
    nrm_ref[...] = normed
    qkv_ref[...] = nn(normed, wq_ref[...]).astype(BF)
    wait_cot()
    dctx_ref[...] = nt(cot_ref[...], wo_ref[...]).astype(BF)
    low, causal = masks()

    def step(pair, carry):
        for g in range(2):
            rows = pl.ds(g * SEQ, SEQ)
            key_pair = qkv_ref[rows, lanes(1, pair)]
            value_pair = qkv_ref[rows, lanes(2, pair)]
            queries = split_heads(low, qkv_ref[rows, lanes(0, pair)])
            soft = attention(low, causal, queries, key_pair)
            soft_b = soft.astype(BF)
            ctx_ref[rows, lanes(0, pair)] = nn(side_by_side(soft_b), split_heads(low, value_pair)).astype(BF)
            dctx = split_heads(low, dctx_ref[rows, lanes(0, pair)])
            dsoft = nt(dctx, value_pair)
            dqkv_ref[rows, lanes(2, pair)] = tn(soft_b, dctx).astype(BF)
            dscore = soft * (dsoft - jnp.sum(soft * dsoft, axis=-1, keepdims=True))
            dscore = (dscore * 0.125).astype(BF)
            dqkv_ref[rows, lanes(0, pair)] = nn(side_by_side(dscore), split_heads(low, key_pair)).astype(BF)
            dqkv_ref[rows, lanes(1, pair)] = tn(dscore, queries).astype(BF)
        return carry

    lax.fori_loop(0, PAIRS, step, 0)


def input_cotangent(x_ref, cot_ref, wq_ref, dqkv_ref, out_ref):
    x = x_ref[...].astype(F32)
    factor, _ = normalise(x)
    dnormed = nt(dqkv_ref[...], wq_ref[...]).astype(BF).astype(F32)
    along = jnp.mean(dnormed * x, axis=-1, keepdims=True)
    dx = factor * dnormed - x * (factor * factor * factor * along)
    out_ref[...] = (cot_ref[...].astype(F32) + dx).astype(BF)


def kernel(
    wq_in, wo_in, act_in, cot_in, stash_in, arr_in, head_in,
    hgq, hgo, na, nc,
    wq, wo, xs, cs, st, fo, bo, qkv, ctx, dctx, dqkv, nrm, accq, acco,
    gsq, gso, grq, gro, g2q, g2o,
    s_w, r_w, s_f, r_f, s_x, r_x, s_c, r_c, s_st, r_st,
    s_fr, s_br, s_ff, r_ff, s_bf, r_bf, s_g1, r_g1, s_g2, r_g2, s_lo, ans_relay, ans_final,
):
    s = lax.axis_index("section")
    d = lax.axis_index("dp")
    c = lax.rem(s, 2)
    plane = s // 2
    y = d // 4
    x = lax.rem(d, 4)
    lv = x // 2
    lc = lax.rem(x + y + plane, 2)
    home = plane * 2 + lc
    layer = lv * 64 + home
    not_first = layer > 0
    not_last = layer < LAYERS - 1

    def column(number, side):
        place = lax.rem(number, 64)
        return lax.rem(place + place // 2 + side, 2)

    def worker(number, core, side):
        place = lax.rem(number, 64)
        return (place // 2 * 2 + core, side * 4 + number // 64 * 2 + column(number, side))

    def core_of(number):
        return 1 - lax.rem(x + y + lax.rem(number, 64) // 2, 2)

    def same_groups(number):
        return lax.rem(c + plane + lax.rem(number, 64) // 2, 2)

    def other(device):
        return jnp.logical_or(device[0] != s, device[1] != d)

    sibling = (plane * 2 + 1 - c, d)
    kc = core_of(s)
    up = lax.rem(layer + 1, LAYERS)
    down = lax.rem(layer + LAYERS - 1, LAYERS)
    upper = worker(up, same_groups(up), y)
    lower = worker(down, same_groups(down), y)
    group = [y * 4 + 2 * j + lax.rem(1 - c + plane + y, 2) for j in range(2)]
    shard = [yy * 4 + 2 * i + lax.rem(1 - c + plane + yy, 2) for yy in range(2) for i in range(2)]
    sib_shard = [yy * 4 + 2 * i + lax.rem(c + plane + yy, 2) for yy in range(2) for i in range(2)]

    def rows_of(which):
        return pl.ds(pl.multiple_of(which * SHARD, SHARD), SHARD)

    def remote(src, dst, send, recv, device):
        return pltpu.make_async_remote_copy(
            src_ref=src, dst_ref=dst, send_sem=send, recv_sem=recv, device_id=device, device_id_type=MESH
        )

    weight_to = [worker(v * 64 + s, kc, yy) for v in range(2) for yy in range(2)]
    act_to = [worker(v * 64 + s, kc, y) for v in range(2)]
    stash_to = [worker(v * 64 + lax.rem(s + 32, 64), kc, y) for v in range(2)]
    stash_from = [(lax.rem(home + 32, 64), group[j]) for j in range(2)]
    grad_to = [(home, shard[k]) for k in range(4)]
    fwd_to = [(lax.rem(up, 64), group[j]) for j in range(2)]
    bwd_to = [(lax.rem(down, 64), group[j]) for j in range(2)]
    before = [lax.rem(v * 64 + s + LAYERS - 1, LAYERS) for v in range(2)]
    after = [lax.rem(v * 64 + s + 1, LAYERS) for v in range(2)]
    fwd_from = [worker(number, core_of(number), y) for number in before]
    bwd_from = [worker(number, core_of(number), y) for number in after]

    barrier = pltpu.get_barrier_semaphore()

    def greet(device):
        pl.semaphore_signal(barrier, inc=1, device_id=device, device_id_type=MESH)

    greet(sibling)
    for device in grad_to + weight_to + stash_from:
        greet(device)
    greet(lower)
    greeted = 1 + 8 + 2 + 1
    for ours, theirs in zip(fwd_from + bwd_to, fwd_to + bwd_from):
        pl.when(other(ours))(lambda device=ours: greet(device))
        greeted = greeted + other(theirs).astype(jnp.int32)
    pl.semaphore_wait(barrier, greeted)

    def answer(sem, device):
        pl.semaphore_signal(sem, inc=1, device_id=device, device_id_type=MESH)

    answer(ans_relay, upper)
    for device in bwd_from:
        pl.when(other(device))(lambda device=device: answer(ans_final, device))

    slot = y * 2 + x // 2
    mine = rows_of(d)
    pending = []

    def send(*what):
        copy = remote(*what)
        copy.start()
        pending.append(copy)

    for n in range(4):
        v = n // 2
        send(wq_in.at[v, 0], wq.at[mine], s_w.at[n, 0], r_w.at[slot, 0], weight_to[n])
        send(wo_in.at[v, 0], wo.at[mine], s_w.at[n, 1], r_w.at[slot, 1], weight_to[n])
    j_here = x // 2
    seat = pl.ds(pl.multiple_of(j_here * SEQ, SEQ), SEQ)
    for v in range(2):
        send(act_in.at[v, 0, 0], xs.at[0, seat], s_x.at[v], r_x.at[0, j_here], act_to[v])
    for v in range(2):
        send(cot_in.at[v, 0, 0], cs.at[0, seat], s_c.at[v], r_c.at[0, j_here], act_to[v])

    def early(source, buffers, send_sem, recv_sem, device):
        return remote(source.at[0, 0], buffers.at[1, seat], send_sem, recv_sem.at[1, j_here], device)

    first_head = early(arr_in, xs, s_x.at[2], r_x, act_to[0])
    last_head = early(head_in, cs, s_c.at[2], r_c, act_to[1])
    pl.when(s == 0)(first_head.start)
    pl.when(s == 63)(last_head.start)
    def send_stash(t, v):
        send(stash_in.at[t, v, 0, 0], st.at[t, seat], s_st.at[t, v], r_st.at[t, j_here], stash_to[v])

    send_stash(0, 0)
    send_stash(0, 1)

    forwards = []
    for k in range(4):
        rows = rows_of(shard[k])
        for part, ref in ((0, wq), (1, wo)):
            remote(ref.at[rows], ref.at[rows], s_f.at[k, part], r_w.at[k, part], sibling).wait_recv()
            copy = remote(ref.at[rows], ref.at[rows], s_f.at[k, part], r_f.at[k, part], sibling)
            copy.start()
            forwards.append(copy)
    for k in range(4):
        rows = rows_of(sib_shard[k])
        for part, ref in ((0, wq), (1, wo)):
            remote(ref.at[rows], ref.at[rows], s_f.at[k, part], r_f.at[k, part], sibling).wait_recv()

    def half(j):
        return pl.ds(j * SEQ, SEQ)

    def arrive(buffers, recv_sem, t):
        for j in range(2):
            ref = buffers.at[t, half(j)]
            remote(ref, ref, s_lo, recv_sem.at[t, j], sibling).wait_recv()

    def relay(source, buffers, send_sem, recv_sem, device):
        return [
            remote(source.at[0, half(j)], buffers.at[1, half(j)], send_sem.at[j], recv_sem.at[1, j], device)
            for j in range(2)
        ]

    def finish(source, landing, send_sem, recv_sem, devices, number):
        round_ = number // 64
        for j in range(2):
            src = source.at[1, half(j)]
            dst = landing.at[round_]
            copy = remote(src, dst, send_sem.at[j], recv_sem.at[round_], devices[j])
            own = pltpu.make_async_copy(src, dst, recv_sem.at[round_])
            yield copy, own, other(devices[j])

    def start_all(copies, allowed):
        for copy, own, away in copies:
            pl.when(jnp.logical_and(allowed, away))(copy.start)
            pl.when(jnp.logical_and(allowed, jnp.logical_not(away)))(own.start)

    fwd_relay = relay(fo, xs, s_fr, r_x, upper)
    bwd_relay = relay(bo, cs, s_br, r_c, lower)
    fwd_final = list(finish(fo, na, s_ff, r_ff, fwd_to, up))
    bwd_final = list(finish(bo, nc, s_bf, r_bf, bwd_to, down))

    def both(copies, allowed, what):
        def act():
            for copy in copies:
                getattr(copy, what)()

        pl.when(allowed)(act)

    def arrive_cot(t):
        return lambda: arrive(cs, r_c, t)

    work = (wq, wo, qkv, ctx, dctx, dqkv, nrm)

    arrive(xs, r_x, 0)
    forward(xs.at[0], wq, wo, qkv, ctx, fo.at[0])
    both(fwd_relay, not_last, "start")
    send_stash(1, 0)
    arrive(st, r_st, 0)
    backward(st.at[0], cs.at[0], arrive_cot(0), *work)
    input_cotangent(st.at[0], cs.at[0], wq, dqkv, bo.at[0])
    pl.semaphore_wait(ans_relay, 1)
    both(bwd_relay, not_first, "start")
    send_stash(1, 1)
    acco[...] = tn(ctx[...], cs[0])
    accq[...] = tn(nrm[...], dqkv[...])

    arrive(xs, r_x, 1)
    forward(xs.at[1], wq, wo, qkv, ctx, fo.at[1])
    start_all(fwd_final, not_last)
    arrive(st, r_st, 1)
    backward(st.at[1], cs.at[1], arrive_cot(1), *work)
    acco[...] += tn(ctx[...], cs[1])
    accq[...] += tn(nrm[...], dqkv[...])

    for k in range(4):
        rows = rows_of(sib_shard[k])
        gsq[k] = accq[rows, :].astype(BF)
        gso[k] = acco[rows, :].astype(BF)
        send(gsq.at[k], grq.at[k], s_g1.at[k, 0], r_g1.at[k, 0], sibling)
        send(gso.at[k], gro.at[k], s_g1.at[k, 1], r_g1.at[k, 1], sibling)
    for k in range(4):
        rows = rows_of(shard[k])
        remote(gsq.at[k], grq.at[k], s_g1.at[k, 0], r_g1.at[k, 0], sibling).wait_recv()
        remote(gso.at[k], gro.at[k], s_g1.at[k, 1], r_g1.at[k, 1], sibling).wait_recv()
        g2q[k] = (accq[rows, :] + grq[k].astype(F32)).astype(BF)
        g2o[k] = (acco[rows, :] + gro[k].astype(F32)).astype(BF)
        send(g2q.at[k], hgq.at[lv, y], s_g2.at[k, 0], r_g2.at[lv, y, 0], grad_to[k])
        send(g2o.at[k], hgo.at[lv, y], s_g2.at[k, 1], r_g2.at[lv, y, 1], grad_to[k])

    input_cotangent(st.at[1], cs.at[1], wq, dqkv, bo.at[1])
    pl.semaphore_wait(ans_final, sum(other(device).astype(jnp.int32) for device in bwd_to))
    start_all(bwd_final, not_first)

    own_arrival = pltpu.make_async_copy(arr_in.at[1, 0], na.at[0], r_ff.at[0])
    own_head = pltpu.make_async_copy(head_in.at[1, 0], nc.at[1], r_bf.at[1])
    pl.when(s == 0)(own_arrival.start)
    pl.when(s == 63)(own_head.start)
    for v in range(2):
        pltpu.make_async_copy(arr_in.at[1, 0], na.at[v], r_ff.at[v]).wait()
        pltpu.make_async_copy(head_in.at[1, 0], nc.at[v], r_bf.at[v]).wait()
    for v in range(2):
        for yy in range(2):
            remote(g2q.at[0], hgq.at[v, yy], s_g2.at[0, 0], r_g2.at[v, yy, 0], sibling).wait_recv()
            remote(g2o.at[0], hgo.at[v, yy], s_g2.at[0, 1], r_g2.at[v, yy, 1], sibling).wait_recv()

    for copy in pending + forwards:
        copy.wait_send()
    pl.when(s == 0)(first_head.wait_send)
    pl.when(s == 63)(last_head.wait_send)
    both(fwd_relay, not_last, "wait_send")
    both(bwd_relay, not_first, "wait_send")
    for copies, allowed in ((fwd_final, not_last), (bwd_final, not_first)):
        for copy, own, away in copies:
            pl.when(jnp.logical_and(allowed, away))(copy.wait_send)


def hand_over(hgq, hgo, na, nc, qkv_grad, out_grad, new_act, new_cot):
    for v in range(2):
        qkv_grad[v, 0] = hgq[v, 0].astype(F32) + hgq[v, 1].astype(F32)
        out_grad[v, 0] = hgo[v, 0].astype(F32) + hgo[v, 1].astype(F32)
        new_act[v, 0, 0] = na[v]
        new_cot[v, 0, 0] = nc[v]


def shards(qkv_weight, out_weight, activations, cotangents, mirrored_stash, arrivals, head_grads):
    dma = pltpu.SemaphoreType.DMA
    hbm = pl.BlockSpec(memory_space=pl.ANY)
    vmem = pl.BlockSpec(memory_space=pltpu.VMEM)
    results = pl.pallas_call(
        kernel,
        out_shape=(
            jax.ShapeDtypeStruct((2, 2, SHARD, 3 * D), BF),
            jax.ShapeDtypeStruct((2, 2, SHARD, D), BF),
            jax.ShapeDtypeStruct((2, SEQ, D), BF),
            jax.ShapeDtypeStruct((2, SEQ, D), BF),
        ),
        in_specs=[hbm] * 7,
        out_specs=[hbm] * 4,
        scratch_shapes=[
            pltpu.VMEM((D, 3 * D), BF),
            pltpu.VMEM((D, D), BF),
            pltpu.VMEM((2, 2 * SEQ, D), BF),
            pltpu.VMEM((2, 2 * SEQ, D), BF),
            pltpu.VMEM((2, 2 * SEQ, D), BF),
            pltpu.VMEM((2, 2 * SEQ, D), BF),
            pltpu.VMEM((2, 2 * SEQ, D), BF),
            pltpu.VMEM((2 * SEQ, 3 * D), BF),
            pltpu.VMEM((2 * SEQ, D), BF),
            pltpu.VMEM((2 * SEQ, D), BF),
            pltpu.VMEM((2 * SEQ, 3 * D), BF),
            pltpu.VMEM((2 * SEQ, D), BF),
            pltpu.VMEM((D, 3 * D), F32),
            pltpu.VMEM((D, D), F32),
            pltpu.VMEM((4, SHARD, 3 * D), BF),
            pltpu.VMEM((4, SHARD, D), BF),
            pltpu.VMEM((4, SHARD, 3 * D), BF),
            pltpu.VMEM((4, SHARD, D), BF),
            pltpu.VMEM((4, SHARD, 3 * D), BF),
            pltpu.VMEM((4, SHARD, D), BF),
            dma((4, 2)), dma((4, 2)),
            dma((4, 2)), dma((4, 2)),
            dma((3,)), dma((2, 2)),
            dma((3,)), dma((2, 2)),
            dma((2, 2)), dma((2, 2)),
            dma((2,)), dma((2,)),
            dma((2,)), dma((2,)),
            dma((2,)), dma((2,)),
            dma((4, 2)), dma((4, 2)),
            dma((4, 2)), dma((2, 2, 2)),
            dma,
            pltpu.SemaphoreType.REGULAR,
            pltpu.SemaphoreType.REGULAR,
        ],
        compiler_params=pltpu.CompilerParams(
            collective_id=0, has_side_effects=True, vmem_limit_bytes=62 * 1024 * 1024
        ),
        cost_estimate=pl.CostEstimate(flops=5_000_000_000, bytes_accessed=8_000_000, transcendentals=2_000_000),
        name="window",
    )(qkv_weight, out_weight, activations, cotangents, mirrored_stash, arrivals, head_grads)
    return pl.pallas_call(
        hand_over,
        out_shape=(
            jax.ShapeDtypeStruct((2, 1, SHARD, 3 * D), F32),
            jax.ShapeDtypeStruct((2, 1, SHARD, D), F32),
            jax.ShapeDtypeStruct((2, 1, 1, SEQ, D), BF),
            jax.ShapeDtypeStruct((2, 1, 1, SEQ, D), BF),
        ),
        in_specs=[vmem] * 4,
        out_specs=[vmem] * 4,
        name="hand_over",
    )(*results)


def solution(mesh):
    return jax.shard_map(
        shards,
        mesh=mesh,
        in_specs=(
            P(None, "section", "dp", None),
            P(None, "section", "dp", None),
            P(None, "section", "dp", None, None),
            P(None, "section", "dp", None, None),
            P(None, None, "section", "dp", None, None),
            P(None, "dp", None, None),
            P(None, "dp", None, None),
        ),
        out_specs=(
            P(None, "section", "dp", None),
            P(None, "section", "dp", None),
            P(None, "section", "dp", None, None),
            P(None, "section", "dp", None, None),
        ),
        check_vma=False,
    )
```

```python
import jax
import jax.numpy as jnp
from jax import lax
from jax.experimental import pallas as pl
from jax.experimental.pallas import tpu as pltpu
from jax.sharding import PartitionSpec as P

MESH = pl.DeviceIdType.MESH
BF = jnp.bfloat16
F32 = jnp.float32
D = 512
SEQ = 128
PAIRS = 4
SHARD = 64
LAYERS = 128


def nn(a, b):
    return lax.dot_general(a, b, (((1,), (0,)), ((), ())), preferred_element_type=F32)


def nt(a, b):
    return lax.dot_general(a, b, (((1,), (1,)), ((), ())), preferred_element_type=F32)


def tn(a, b):
    return lax.dot_general(a, b, (((0,), (0,)), ((), ())), preferred_element_type=F32)


def normalise(x):
    factor = lax.rsqrt(jnp.mean(x * x, axis=-1, keepdims=True) + 1e-05)
    return factor, (x * factor).astype(BF)


def split_heads(low, pair):
    zero = jnp.zeros_like(pair)
    return jnp.concatenate([jnp.where(low, pair, zero), jnp.where(low, zero, pair)], axis=0)


def side_by_side(both):
    return jnp.concatenate([both[:SEQ], both[SEQ:]], axis=1)


def masks():
    low = lax.broadcasted_iota(jnp.int32, (SEQ, SEQ), 1) < 64
    row = lax.broadcasted_iota(jnp.int32, (2 * SEQ, SEQ), 0)
    col = lax.broadcasted_iota(jnp.int32, (2 * SEQ, SEQ), 1)
    return low, col <= lax.rem(row, SEQ)


def attention(low, causal, queries, keys):
    scores = nt(queries, keys) * 0.125
    raised = jnp.where(causal, jnp.exp(scores), 0.0)
    return raised * (1.0 / jnp.sum(raised, axis=-1, keepdims=True))


def lanes(part, pair):
    return pl.ds(pl.multiple_of(part * D + pair * SEQ, SEQ), SEQ)


def forward(x_ref, wq_ref, wo_ref, qkv_ref, ctx_ref, out_ref):
    x = x_ref[...].astype(F32)
    _, normed = normalise(x)
    qkv_ref[...] = nn(normed, wq_ref[...]).astype(BF)
    low, causal = masks()

    def step(pair, carry):
        for g in range(2):
            rows = pl.ds(g * SEQ, SEQ)
            queries = split_heads(low, qkv_ref[rows, lanes(0, pair)])
            soft = attention(low, causal, queries, qkv_ref[rows, lanes(1, pair)]).astype(BF)
            values = split_heads(low, qkv_ref[rows, lanes(2, pair)])
            ctx_ref[rows, lanes(0, pair)] = nn(side_by_side(soft), values).astype(BF)
        return carry

    lax.fori_loop(0, PAIRS, step, 0, unroll=True)
    out_ref[...] = (x + nn(ctx_ref[...], wo_ref[...])).astype(BF)


def backward(x_ref, cot_ref, wait_cot, wq_ref, wo_ref, qkv_ref, ctx_ref, dctx_ref, dqkv_ref, nrm_ref):
    _, normed = normalise(x_ref[...].astype(F32))
    nrm_ref[...] = normed
    qkv_ref[...] = nn(normed, wq_ref[...]).astype(BF)
    wait_cot()
    dctx_ref[...] = nt(cot_ref[...], wo_ref[...]).astype(BF)
    low, causal = masks()

    def step(pair, carry):
        for g in range(2):
            rows = pl.ds(g * SEQ, SEQ)
            key_pair = qkv_ref[rows, lanes(1, pair)]
            value_pair = qkv_ref[rows, lanes(2, pair)]
            queries = split_heads(low, qkv_ref[rows, lanes(0, pair)])
            soft = attention(low, causal, queries, key_pair)
            soft_b = soft.astype(BF)
            ctx_ref[rows, lanes(0, pair)] = nn(side_by_side(soft_b), split_heads(low, value_pair)).astype(BF)
            dctx = split_heads(low, dctx_ref[rows, lanes(0, pair)])
            dsoft = nt(dctx, value_pair)
            dqkv_ref[rows, lanes(2, pair)] = tn(soft_b, dctx).astype(BF)
            dscore = soft * (dsoft - jnp.sum(soft * dsoft, axis=-1, keepdims=True))
            dscore = (dscore * 0.125).astype(BF)
            dqkv_ref[rows, lanes(0, pair)] = nn(side_by_side(dscore), split_heads(low, key_pair)).astype(BF)
            dqkv_ref[rows, lanes(1, pair)] = tn(dscore, queries).astype(BF)
        return carry

    lax.fori_loop(0, PAIRS, step, 0, unroll=True)


def input_cotangent(x_ref, cot_ref, wq_ref, dqkv_ref, out_ref):
    x = x_ref[...].astype(F32)
    factor, _ = normalise(x)
    dnormed = nt(dqkv_ref[...], wq_ref[...]).astype(BF).astype(F32)
    along = jnp.mean(dnormed * x, axis=-1, keepdims=True)
    dx = factor * dnormed - x * (factor * factor * factor * along)
    out_ref[...] = (cot_ref[...].astype(F32) + dx).astype(BF)


def kernel(
    wq_in, wo_in, act_in, cot_in, stash_in, arr_in, head_in,
    hgq, hgo, na, nc,
    wq, wo, xs, cs, st, fo, bo, qkv, ctx, dctx, dqkv, nrm, accq, acco,
    gsq, gso, grq, gro, g2q, g2o,
    s_w, r_w, s_f, r_f, s_x, r_x, s_c, r_c, s_st, r_st,
    s_fr, s_br, s_ff, r_ff, s_bf, r_bf, s_g1, r_g1, s_g2, r_g2, s_lo, ans_relay, ans_final,
):
    s = lax.axis_index("section")
    d = lax.axis_index("dp")
    c = lax.rem(s, 2)
    plane = s // 2
    y = d // 4
    x = lax.rem(d, 4)
    lv = x // 2
    lc = lax.rem(x + y + plane, 2)
    home = plane * 2 + lc
    layer = lv * 64 + home
    not_first = layer > 0
    not_last = layer < LAYERS - 1

    def column(number, side):
        place = lax.rem(number, 64)
        return lax.rem(place + place // 2 + side, 2)

    def worker(number, core, side):
        place = lax.rem(number, 64)
        return (place // 2 * 2 + core, side * 4 + number // 64 * 2 + column(number, side))

    def core_of(number):
        return 1 - lax.rem(x + y + lax.rem(number, 64) // 2, 2)

    def same_groups(number):
        return lax.rem(c + plane + lax.rem(number, 64) // 2, 2)

    def other(device):
        return jnp.logical_or(device[0] != s, device[1] != d)

    sibling = (plane * 2 + 1 - c, d)
    kc = core_of(s)
    up = lax.rem(layer + 1, LAYERS)
    down = lax.rem(layer + LAYERS - 1, LAYERS)
    upper = worker(up, same_groups(up), y)
    lower = worker(down, same_groups(down), y)
    group = [y * 4 + 2 * j + lax.rem(1 - c + plane + y, 2) for j in range(2)]
    shard = [yy * 4 + 2 * i + lax.rem(1 - c + plane + yy, 2) for yy in range(2) for i in range(2)]
    sib_shard = [yy * 4 + 2 * i + lax.rem(c + plane + yy, 2) for yy in range(2) for i in range(2)]

    def rows_of(which):
        return pl.ds(pl.multiple_of(which * SHARD, SHARD), SHARD)

    def remote(src, dst, send, recv, device):
        return pltpu.make_async_remote_copy(
            src_ref=src, dst_ref=dst, send_sem=send, recv_sem=recv, device_id=device, device_id_type=MESH
        )

    weight_to = [worker(v * 64 + s, kc, yy) for v in range(2) for yy in range(2)]
    act_to = [worker(v * 64 + s, kc, y) for v in range(2)]
    stash_to = [worker(v * 64 + lax.rem(s + 32, 64), kc, y) for v in range(2)]
    stash_from = [(lax.rem(home + 32, 64), group[j]) for j in range(2)]
    grad_to = [(home, shard[k]) for k in range(4)]
    fwd_to = [(lax.rem(up, 64), group[j]) for j in range(2)]
    bwd_to = [(lax.rem(down, 64), group[j]) for j in range(2)]
    before = [lax.rem(v * 64 + s + LAYERS - 1, LAYERS) for v in range(2)]
    after = [lax.rem(v * 64 + s + 1, LAYERS) for v in range(2)]
    fwd_from = [worker(number, core_of(number), y) for number in before]
    bwd_from = [worker(number, core_of(number), y) for number in after]

    barrier = pltpu.get_barrier_semaphore()

    def greet(device):
        pl.semaphore_signal(barrier, inc=1, device_id=device, device_id_type=MESH)

    greet(sibling)
    for device in grad_to + weight_to + stash_from:
        greet(device)
    greet(lower)
    greeted = 1 + 8 + 2 + 1
    for ours, theirs in zip(fwd_from + bwd_to, fwd_to + bwd_from):
        pl.when(other(ours))(lambda device=ours: greet(device))
        greeted = greeted + other(theirs).astype(jnp.int32)
    pl.semaphore_wait(barrier, greeted)

    def answer(sem, device):
        pl.semaphore_signal(sem, inc=1, device_id=device, device_id_type=MESH)

    answer(ans_relay, upper)
    for device in bwd_from:
        pl.when(other(device))(lambda device=device: answer(ans_final, device))

    slot = y * 2 + x // 2
    mine = rows_of(d)
    pending = []

    def send(*what):
        copy = remote(*what)
        copy.start()
        pending.append(copy)

    for n in range(4):
        v = n // 2
        send(wq_in.at[v, 0], wq.at[mine], s_w.at[n, 0], r_w.at[slot, 0], weight_to[n])
        send(wo_in.at[v, 0], wo.at[mine], s_w.at[n, 1], r_w.at[slot, 1], weight_to[n])
    j_here = x // 2
    seat = pl.ds(pl.multiple_of(j_here * SEQ, SEQ), SEQ)
    for v in range(2):
        send(act_in.at[v, 0, 0], xs.at[0, seat], s_x.at[v], r_x.at[0, j_here], act_to[v])
    for v in range(2):
        send(cot_in.at[v, 0, 0], cs.at[0, seat], s_c.at[v], r_c.at[0, j_here], act_to[v])

    def early(source, buffers, send_sem, recv_sem, device):
        return remote(source.at[0, 0], buffers.at[1, seat], send_sem, recv_sem.at[1, j_here], device)

    first_head = early(arr_in, xs, s_x.at[2], r_x, act_to[0])
    last_head = early(head_in, cs, s_c.at[2], r_c, act_to[1])
    pl.when(s == 0)(first_head.start)
    pl.when(s == 63)(last_head.start)
    def send_stash(t, v):
        send(stash_in.at[t, v, 0, 0], st.at[t, seat], s_st.at[t, v], r_st.at[t, j_here], stash_to[v])

    send_stash(0, 0)
    send_stash(0, 1)

    forwards = []
    for k in range(4):
        rows = rows_of(shard[k])
        for part, ref in ((0, wq), (1, wo)):
            remote(ref.at[rows], ref.at[rows], s_f.at[k, part], r_w.at[k, part], sibling).wait_recv()
            copy = remote(ref.at[rows], ref.at[rows], s_f.at[k, part], r_f.at[k, part], sibling)
            copy.start()
            forwards.append(copy)
    for k in range(4):
        rows = rows_of(sib_shard[k])
        for part, ref in ((0, wq), (1, wo)):
            remote(ref.at[rows], ref.at[rows], s_f.at[k, part], r_f.at[k, part], sibling).wait_recv()

    def half(j):
        return pl.ds(j * SEQ, SEQ)

    def arrive(buffers, recv_sem, t):
        for j in range(2):
            ref = buffers.at[t, half(j)]
            remote(ref, ref, s_lo, recv_sem.at[t, j], sibling).wait_recv()

    def relay(source, buffers, send_sem, recv_sem, device):
        return [
            remote(source.at[0, half(j)], buffers.at[1, half(j)], send_sem.at[j], recv_sem.at[1, j], device)
            for j in range(2)
        ]

    def finish(source, landing, send_sem, recv_sem, devices, number):
        round_ = number // 64
        for j in range(2):
            src = source.at[1, half(j)]
            dst = landing.at[round_]
            copy = remote(src, dst, send_sem.at[j], recv_sem.at[round_], devices[j])
            own = pltpu.make_async_copy(src, dst, recv_sem.at[round_])
            yield copy, own, other(devices[j])

    def start_all(copies, allowed):
        for copy, own, away in copies:
            pl.when(jnp.logical_and(allowed, away))(copy.start)
            pl.when(jnp.logical_and(allowed, jnp.logical_not(away)))(own.start)

    fwd_relay = relay(fo, xs, s_fr, r_x, upper)
    bwd_relay = relay(bo, cs, s_br, r_c, lower)
    fwd_final = list(finish(fo, na, s_ff, r_ff, fwd_to, up))
    bwd_final = list(finish(bo, nc, s_bf, r_bf, bwd_to, down))

    def both(copies, allowed, what):
        def act():
            for copy in copies:
                getattr(copy, what)()

        pl.when(allowed)(act)

    def arrive_cot(t):
        return lambda: arrive(cs, r_c, t)

    work = (wq, wo, qkv, ctx, dctx, dqkv, nrm)

    arrive(xs, r_x, 0)
    forward(xs.at[0], wq, wo, qkv, ctx, fo.at[0])
    both(fwd_relay, not_last, "start")
    send_stash(1, 0)
    arrive(st, r_st, 0)
    backward(st.at[0], cs.at[0], arrive_cot(0), *work)
    input_cotangent(st.at[0], cs.at[0], wq, dqkv, bo.at[0])
    pl.semaphore_wait(ans_relay, 1)
    both(bwd_relay, not_first, "start")
    send_stash(1, 1)
    acco[...] = tn(ctx[...], cs[0])
    accq[...] = tn(nrm[...], dqkv[...])

    arrive(xs, r_x, 1)
    forward(xs.at[1], wq, wo, qkv, ctx, fo.at[1])
    start_all(fwd_final, not_last)
    arrive(st, r_st, 1)
    backward(st.at[1], cs.at[1], arrive_cot(1), *work)
    acco[...] += tn(ctx[...], cs[1])
    accq[...] += tn(nrm[...], dqkv[...])

    for k in range(4):
        rows = rows_of(sib_shard[k])
        gsq[k] = accq[rows, :].astype(BF)
        gso[k] = acco[rows, :].astype(BF)
        send(gsq.at[k], grq.at[k], s_g1.at[k, 0], r_g1.at[k, 0], sibling)
        send(gso.at[k], gro.at[k], s_g1.at[k, 1], r_g1.at[k, 1], sibling)
    for k in range(4):
        rows = rows_of(shard[k])
        remote(gsq.at[k], grq.at[k], s_g1.at[k, 0], r_g1.at[k, 0], sibling).wait_recv()
        remote(gso.at[k], gro.at[k], s_g1.at[k, 1], r_g1.at[k, 1], sibling).wait_recv()
        g2q[k] = (accq[rows, :] + grq[k].astype(F32)).astype(BF)
        g2o[k] = (acco[rows, :] + gro[k].astype(F32)).astype(BF)
        send(g2q.at[k], hgq.at[lv, y], s_g2.at[k, 0], r_g2.at[lv, y, 0], grad_to[k])
        send(g2o.at[k], hgo.at[lv, y], s_g2.at[k, 1], r_g2.at[lv, y, 1], grad_to[k])

    input_cotangent(st.at[1], cs.at[1], wq, dqkv, bo.at[1])
    pl.semaphore_wait(ans_final, sum(other(device).astype(jnp.int32) for device in bwd_to))
    start_all(bwd_final, not_first)

    own_arrival = pltpu.make_async_copy(arr_in.at[1, 0], na.at[0], r_ff.at[0])
    own_head = pltpu.make_async_copy(head_in.at[1, 0], nc.at[1], r_bf.at[1])
    pl.when(s == 0)(own_arrival.start)
    pl.when(s == 63)(own_head.start)
    for v in range(2):
        pltpu.make_async_copy(arr_in.at[1, 0], na.at[v], r_ff.at[v]).wait()
        pltpu.make_async_copy(head_in.at[1, 0], nc.at[v], r_bf.at[v]).wait()
    for v in range(2):
        for yy in range(2):
            remote(g2q.at[0], hgq.at[v, yy], s_g2.at[0, 0], r_g2.at[v, yy, 0], sibling).wait_recv()
            remote(g2o.at[0], hgo.at[v, yy], s_g2.at[0, 1], r_g2.at[v, yy, 1], sibling).wait_recv()

    for copy in pending + forwards:
        copy.wait_send()
    pl.when(s == 0)(first_head.wait_send)
    pl.when(s == 63)(last_head.wait_send)
    both(fwd_relay, not_last, "wait_send")
    both(bwd_relay, not_first, "wait_send")
    for copies, allowed in ((fwd_final, not_last), (bwd_final, not_first)):
        for copy, own, away in copies:
            pl.when(jnp.logical_and(allowed, away))(copy.wait_send)


def hand_over(hgq, hgo, na, nc, qkv_grad, out_grad, new_act, new_cot):
    for v in range(2):
        qkv_grad[v, 0] = hgq[v, 0].astype(F32) + hgq[v, 1].astype(F32)
        out_grad[v, 0] = hgo[v, 0].astype(F32) + hgo[v, 1].astype(F32)
        new_act[v, 0, 0] = na[v]
        new_cot[v, 0, 0] = nc[v]


def shards(qkv_weight, out_weight, activations, cotangents, mirrored_stash, arrivals, head_grads):
    dma = pltpu.SemaphoreType.DMA
    hbm = pl.BlockSpec(memory_space=pl.ANY)
    vmem = pl.BlockSpec(memory_space=pltpu.VMEM)
    results = pl.pallas_call(
        kernel,
        out_shape=(
            jax.ShapeDtypeStruct((2, 2, SHARD, 3 * D), BF),
            jax.ShapeDtypeStruct((2, 2, SHARD, D), BF),
            jax.ShapeDtypeStruct((2, SEQ, D), BF),
            jax.ShapeDtypeStruct((2, SEQ, D), BF),
        ),
        in_specs=[hbm] * 7,
        out_specs=[hbm] * 4,
        scratch_shapes=[
            pltpu.VMEM((D, 3 * D), BF),
            pltpu.VMEM((D, D), BF),
            pltpu.VMEM((2, 2 * SEQ, D), BF),
            pltpu.VMEM((2, 2 * SEQ, D), BF),
            pltpu.VMEM((2, 2 * SEQ, D), BF),
            pltpu.VMEM((2, 2 * SEQ, D), BF),
            pltpu.VMEM((2, 2 * SEQ, D), BF),
            pltpu.VMEM((2 * SEQ, 3 * D), BF),
            pltpu.VMEM((2 * SEQ, D), BF),
            pltpu.VMEM((2 * SEQ, D), BF),
            pltpu.VMEM((2 * SEQ, 3 * D), BF),
            pltpu.VMEM((2 * SEQ, D), BF),
            pltpu.VMEM((D, 3 * D), F32),
            pltpu.VMEM((D, D), F32),
            pltpu.VMEM((4, SHARD, 3 * D), BF),
            pltpu.VMEM((4, SHARD, D), BF),
            pltpu.VMEM((4, SHARD, 3 * D), BF),
            pltpu.VMEM((4, SHARD, D), BF),
            pltpu.VMEM((4, SHARD, 3 * D), BF),
            pltpu.VMEM((4, SHARD, D), BF),
            dma((4, 2)), dma((4, 2)),
            dma((4, 2)), dma((4, 2)),
            dma((3,)), dma((2, 2)),
            dma((3,)), dma((2, 2)),
            dma((2, 2)), dma((2, 2)),
            dma((2,)), dma((2,)),
            dma((2,)), dma((2,)),
            dma((2,)), dma((2,)),
            dma((4, 2)), dma((4, 2)),
            dma((4, 2)), dma((2, 2, 2)),
            dma,
            pltpu.SemaphoreType.REGULAR,
            pltpu.SemaphoreType.REGULAR,
        ],
        compiler_params=pltpu.CompilerParams(
            collective_id=0, has_side_effects=True, vmem_limit_bytes=62 * 1024 * 1024
        ),
        cost_estimate=pl.CostEstimate(flops=5_000_000_000, bytes_accessed=8_000_000, transcendentals=2_000_000),
        name="window",
    )(qkv_weight, out_weight, activations, cotangents, mirrored_stash, arrivals, head_grads)
    return pl.pallas_call(
        hand_over,
        out_shape=(
            jax.ShapeDtypeStruct((2, 1, SHARD, 3 * D), F32),
            jax.ShapeDtypeStruct((2, 1, SHARD, D), F32),
            jax.ShapeDtypeStruct((2, 1, 1, SEQ, D), BF),
            jax.ShapeDtypeStruct((2, 1, 1, SEQ, D), BF),
        ),
        in_specs=[vmem] * 4,
        out_specs=[vmem] * 4,
        name="hand_over",
    )(*results)


def solution(mesh):
    return jax.shard_map(
        shards,
        mesh=mesh,
        in_specs=(
            P(None, "section", "dp", None),
            P(None, "section", "dp", None),
            P(None, "section", "dp", None, None),
            P(None, "section", "dp", None, None),
            P(None, None, "section", "dp", None, None),
            P(None, "dp", None, None),
            P(None, "dp", None, None),
        ),
        out_specs=(
            P(None, "section", "dp", None),
            P(None, "section", "dp", None),
            P(None, "section", "dp", None, None),
            P(None, "section", "dp", None, None),
        ),
        check_vma=False,
    )
```
